32 devices in a mesh: section: 2 (over core), dp: 16 (over z, y, x).
Axes of the slice: x: 2, y: 2, z: 4, core: 2. Of those that a mesh axis runs over, the one named last changes fastest.
Arguments:
- ends: bfloat16 [2, 2, 16, 1024, 576], P('section', None, 'dp'), may hold values from -6 to 6
- doc_lengths: int32 [2, 16, 4], P(None, 'dp'), may hold values from 1 to 800, 1024 in all within a row
- norm_gains: bfloat16 [2, 1152], P('section', 'dp'), may hold values from 0.5 to 1.5
- w_qkv: bfloat16 [2, 552960], P('section', 'dp'), may hold values from -0.25 to 0.25
- w_out: bfloat16 [2, 331776], P('section', 'dp'), may hold values from -0.75 to 0.75
- w_gate_up: bfloat16 [2, 1769472], P('section', 'dp'), may hold values from -0.25 to 0.25
- w_down: bfloat16 [2, 884736], P('section', 'dp'), may hold values from -0.3125 to 0.3125
Outputs:
- section_outputs: bfloat16 [2, 2, 16, 1024, 576], P('section', None, 'dp')
- input_grads: float32 [2, 2, 16, 1024, 576], P('section', None, 'dp')
- grad_gains: float32 [2, 1152], P('section', 'dp')
- grad_qkv: float32 [2, 552960], P('section', 'dp')
- grad_out: float32 [2, 331776], P('section', 'dp')
- grad_gate_up: float32 [2, 1769472], P('section', 'dp')
- grad_down: float32 [2, 884736], P('section', 'dp')
The draws below stay inside these ranges and needn't reach their ends.
Inputs may be any that keep to these rules, and one draw needn't show every extreme that they name: `doc_lengths`: in every sequence the 4 lengths sum to 1024 and the largest is 800.
All inputs are finite; a program needn't handle non-finite values.
Results may differ from the reference program's by a relative error of at most 0.023.
Values may be sent and summed in bfloat16 or wider, within the bound.
A program may use at most 320 MiB of HBM per device.

```python
import math
import jax
import jax.numpy as jnp
import numpy as np
from jax import lax

D = 576
H = 9
KV = 3
HD = 64
FF = 1536
LEN = 1024
DOCS = 4
MB = 2
SEQS = 16
QKV = 960
DOC_MOST = 800


def block_scale(key, shape, shards, smallest, high):
    def one(axis_at, shards_of):
        steps = jax.random.uniform(jax.random.fold_in(jax.random.fold_in(key, 6), axis_at), (shards_of,), jnp.float32, smallest / len(shards), high / len(shards))
        return jnp.repeat(jnp.exp(steps), shape[axis_at] // shards_of).reshape((-1,) + (1,) * (len(shape) - axis_at - 1))

    gain = one(*shards[0])
    for cut in shards[1:]:
        gain = gain * one(*cut)
    return gain


def split_up(number_of, total, reach, skew):
    loads = [(1 << 20) // math.isqrt(rank ** skew) + 1 for rank in range(2, number_of + 1)]
    surplus, given = total - reach - (number_of - 1), [1] * (number_of - 1)
    while surplus > 0:
        candidates = [i for i in range(number_of - 1) if given[i] < reach]
        whole, remaining = sum([loads[i] for i in candidates]), surplus
        for i in candidates:
            extra = min(reach - given[i], max(1, remaining * loads[i] // whole), surplus)
            given[i] = given[i] + extra
            surplus = surplus - extra
    return np.array([reach] + given)


def ragged(key, amount, total, reach, slope):
    if amount == 2:
        one = jax.random.randint(key, (), max(1, total - reach), min(reach, total - 1) + 1)
        return jnp.stack([one, total - one])
    sizes = jnp.asarray(split_up(amount, total, reach, slope), jnp.int32)
    couples = (amount - 1) // 2
    source_of, taker = sizes[1:1 + 2 * couples:2], sizes[2:2 + 2 * couples:2]
    margin = jnp.minimum(source_of - 1, reach - taker)
    shifted = jax.random.randint(jax.random.fold_in(key, 1), (couples,), 0, 1 << 20) % (margin + 1)
    sizes = sizes.at[1:1 + 2 * couples:2].set(source_of - shifted).at[2:2 + 2 * couples:2].set(taker + shifted)
    return sizes[jax.random.permutation(jax.random.fold_in(key, 2), amount)]


def gaussian(stream_key, shape, width, most, pieces=(), held_as=jnp.bfloat16):
    factor_of = block_scale(stream_key, shape, pieces, -0.22, 0.18) if pieces else 1.0
    drawn = jax.random.normal(stream_key, shape, jnp.float32) * width * factor_of
    return jnp.minimum(jnp.maximum(drawn, -most), most).astype(held_as)


def setup_inputs(seed: int = 0) -> dict:
    key_of = jax.random.split(jax.random.key(seed), 8)
    return {
        "ends": gaussian(key_of[0], (2, MB, SEQS, LEN, D), 1.0, 6.0, ((0, 2), (2, 16))),
        "doc_lengths": jax.vmap(lambda own: ragged(own, DOCS, LEN, DOC_MOST, 2))(jax.random.split(key_of[1], MB * SEQS)).reshape((MB, SEQS, DOCS)).astype(jnp.int32),
        "norm_gains": jnp.clip(1.0 + 0.1 * jax.random.normal(key_of[2], (2, 2 * D), jnp.float32), 0.5, 1.5).astype(jnp.bfloat16),
        "w_qkv": gaussian(key_of[3], (2, D * QKV), D ** -0.5, 0.25, ((0, 2), (1, 16))),
        "w_out": gaussian(key_of[4], (2, H * HD * D), (D // 9) ** -0.5, 0.75, ((0, 2), (1, 16))),
        "w_gate_up": gaussian(key_of[5], (2, 2 * D * FF), D ** -0.5, 0.25, ((0, 2), (1, 16))),
        "w_down": gaussian(key_of[6], (2, FF * D), (FF // 4) ** -0.5, 0.3125, ((0, 2), (1, 16))),
    }


norm_eps = 1e-05
rope_base = 100000.0
masked_score = -1e+30
highest = lax.Precision.HIGHEST

@jax.custom_vjp
def low(v):
    return lax.optimization_barrier(v.astype(jnp.bfloat16)).astype(jnp.float32)

@jax.custom_vjp
def low_back(v):
    return v

def low_keep(v):
    return (low(v), None)

def low_pass(kept, grad):
    return (grad,)

def back_keep(v):
    return (v, None)

def back_low(kept, grad):
    return (low(grad),)
low.defvjp(low_keep, low_pass)
low_back.defvjp(back_keep, back_low)

def doc_layout(lengths):
    bounds = jnp.cumsum(lengths).astype(jnp.int32)
    starts = (bounds - lengths).astype(jnp.int32)
    places = jnp.arange(LEN, dtype=jnp.int32)
    segment = lax.optimization_barrier(jnp.sum((places[:, None] >= bounds[None, :]).astype(jnp.int32), axis=1)).astype(jnp.int32)
    onehot = (segment[:, None] == jnp.arange(DOCS, dtype=jnp.int32)[None, :]).astype(jnp.int32)
    position = (places - lax.optimization_barrier(jnp.sum(onehot * starts[None, :], axis=1))).astype(jnp.int32)
    return (segment, position)

def rope_tables(position):
    half_dim = HD // 2
    inverse = rope_base ** (-(jnp.arange(half_dim, dtype=jnp.float32) * 2.0) / HD)
    angles = position.astype(jnp.float32)[..., None] * inverse
    return (jnp.cos(angles), jnp.sin(angles))

def rotate(values, cosine, sine_part):
    half_dim = values.shape[-1] // 2
    first_half = values[..., :half_dim]
    second_half = values[..., half_dim:]
    cos_heads = cosine[..., None, :]
    sin_heads = sine_part[..., None, :]
    return jnp.concatenate([first_half * cos_heads - second_half * sin_heads, second_half * cos_heads + first_half * sin_heads], axis=-1)

def rms_norm(values, gain_vec):
    return values * lax.rsqrt(lax.optimization_barrier(jnp.mean(values * values, axis=-1, keepdims=True)) + norm_eps) * gain_vec

def product(left_side, right_side):
    return jnp.dot(left_side, right_side, precision=highest, preferred_element_type=jnp.float32)

def attend(queries, key_rows, value_rows, segment):
    group = H // KV
    block_rows = min(512, LEN)
    blocks = LEN // block_rows
    query_blocks = queries.reshape(blocks, block_rows, KV, group, HD)
    starts = jnp.arange(blocks, dtype=jnp.int32) * block_rows
    score_scale = HD ** (-0.5)

    def one_block(block_item):
        query_part, start = block_item
        scores = jnp.einsum('qkgd,tkd->kgqt', query_part, key_rows, precision=highest) * score_scale
        scores = low_back(scores)
        row_ids = start + jnp.arange(block_rows, dtype=jnp.int32)
        query_seg = lax.dynamic_slice_in_dim(segment, start, block_rows)
        allowed = (query_seg[:, None] == segment[None, :]) & (row_ids[:, None] >= jnp.arange(LEN, dtype=jnp.int32)[None, :])
        scores = jnp.where(allowed[None, None], scores, masked_score)
        softmax_p = low(jax.nn.softmax(scores, axis=-1))
        return jnp.einsum('kgqt,tkd->qkgd', softmax_p, value_rows, precision=highest)
    block_outs = lax.map(jax.checkpoint(one_block), (query_blocks, starts))
    return block_outs.reshape(LEN, H * HD)

def layer(layer_in, gains, w_qkv, w_out, w_gate_up, w_down, segment, position):
    hidden_in = low(rms_norm(layer_in, gains[:D]))
    projected = low_back(product(hidden_in, w_qkv))
    cosine, sine_part = rope_tables(position)
    queries = low(rotate(projected[:, :H * HD].reshape(LEN, H, HD), cosine, sine_part))
    key_rows = low(rotate(projected[:, H * HD:(H + KV) * HD].reshape(LEN, KV, HD), cosine, sine_part))
    value_rows = low(projected[:, (H + KV) * HD:].reshape(LEN, KV, HD))
    mixed = low(low_back(attend(queries, key_rows, value_rows, segment)))
    resid = layer_in + low_back(product(mixed, w_out))
    normed = low(rms_norm(resid, gains[D:]))
    gate_up = low_back(product(normed, w_gate_up))
    hidden = low(jax.nn.silu(gate_up[:, :FF]) * gate_up[:, FF:])
    return resid + low_back(product(hidden, w_down))

def reference(ends, doc_lengths, norm_gains, w_qkv, w_out, w_gate_up, w_down):
    segment, position = jax.vmap(jax.vmap(doc_layout))(doc_lengths)
    seg_flat = segment.reshape(MB * SEQS, LEN)
    pos_flat = position.reshape(MB * SEQS, LEN)
    inputs = ends[0].astype(jnp.float32)
    cotangent = ends[1].astype(jnp.float32)
    probe = jnp.zeros_like(inputs)

    def forward(first_in, probe_in, gains_all, qkv_all, out_all, gate_up_all, down_all):

        def run(section_number, section_in):
            params = (gains_all[section_number], qkv_all[section_number].reshape(D, QKV), out_all[section_number].reshape(H * HD, D), gate_up_all[section_number].reshape(D, 2 * FF), down_all[section_number].reshape(FF, D))

            def one_seq(block_item):
                row_data, seg_row, pos_row = block_item
                return layer(row_data, params[0], params[1], params[2], params[3], params[4], seg_row, pos_row)
            row_data = section_in.reshape(MB * SEQS, LEN, D)
            result = lax.map(jax.checkpoint(one_seq), (row_data, seg_flat, pos_flat))
            return result.reshape(MB, SEQS, LEN, D)
        first_out = run(0, first_in)
        second_out = run(1, low_back(low(first_out)) + probe_in)
        return (first_out, second_out)
    floats = (norm_gains.astype(jnp.float32), w_qkv.astype(jnp.float32), w_out.astype(jnp.float32), w_gate_up.astype(jnp.float32), w_down.astype(jnp.float32))
    (first_out, second_out), pullback = jax.vjp(forward, inputs, probe, floats[0], floats[1], floats[2], floats[3], floats[4])
    grads = pullback((jnp.zeros_like(first_out), cotangent))
    section_outputs = jnp.stack([first_out, second_out]).astype(jnp.bfloat16)
    input_grads = jnp.stack([grads[0], grads[1]])
    return (section_outputs, input_grads, grads[2], grads[3], grads[4], grads[5], grads[6])
```

```python
import jax
import jax.numpy as jnp
import numpy as np
from jax import lax
from jax.experimental import pallas as pl
from jax.experimental.pallas import tpu as pltpu
from jax.sharding import PartitionSpec as P

D = 576
H = 9
KV = 3
HD = 64
FF = 1536
LEN = 1024
DOCS = 4
GROUP = H // KV
QKV = (H + 2 * KV) * HD
ROT = (H + KV) * HD
BLOCK = 256
BLOCKS = LEN // BLOCK
FF_PART = 512

norm_eps = 1e-05
rope_base = 100000.0
masked_score = -1e30
score_scale = HD ** (-0.5)
bf16 = jnp.bfloat16
f32 = jnp.float32
vmem_bytes = 60 * 2**20


def dot(left, right):
    return jnp.dot(left, right, preferred_element_type=f32)


def dot_rows(left, right):
    return lax.dot_general(left, right, (((0,), (0,)), ((), ())), preferred_element_type=f32)


def dot_cols(left, right):
    return lax.dot_general(left, right, (((1,), (1,)), ((), ())), preferred_element_type=f32)


def doc_layout(lengths):
    bounds = jnp.cumsum(lengths)
    starts = bounds - lengths
    places = jnp.arange(LEN, dtype=jnp.int32)
    segment = jnp.sum((places[:, None] >= bounds[None, :]).astype(jnp.int32), axis=1)
    onehot = (segment[:, None] == jnp.arange(DOCS, dtype=jnp.int32)[None, :]).astype(jnp.int32)
    position = places - jnp.sum(onehot * starts[None, :], axis=1)
    return (segment, position)


def rope_tables(position):
    half = HD // 2
    inverse = rope_base ** (-(jnp.arange(half, dtype=f32) * 2.0) / HD)
    angles = position.astype(f32)[:, None] * inverse
    cosine, sine = jnp.cos(angles), jnp.sin(angles)
    return (
        jnp.concatenate([cosine] * 4, axis=1),
        jnp.concatenate([-sine, sine, -sine, sine], axis=1),
    )


def norm(values):
    inverse = lax.rsqrt(jnp.mean(values * values, axis=-1, keepdims=True) + norm_eps)
    return values * inverse, inverse


def norm_back(grad, normed, inverse, gain):
    scaled = grad * gain
    return inverse * (scaled - normed * jnp.mean(scaled * normed, axis=-1, keepdims=True))


def swap_halves(pair):
    lane = lax.broadcasted_iota(jnp.int32, pair.shape, 1)
    ahead = pltpu.roll(pair, 2 * HD - HD // 2, 1)
    behind = pltpu.roll(pair, HD // 2, 1)
    return jnp.where(lane % HD < HD // 2, ahead, behind)


def attention_bias(seg_col, seg_row, block):
    width = (block + 1) * BLOCK
    rows = block * BLOCK + lax.broadcasted_iota(jnp.int32, (BLOCK, width), 0)
    cols = lax.broadcasted_iota(jnp.int32, (BLOCK, width), 1)
    allowed = (seg_col == seg_row) & (rows >= cols)
    return jnp.where(allowed, 0.0, masked_score)


def group_heads(ref, rows, group):
    first = group * GROUP
    return jnp.concatenate(
        [ref[rows, (first + j) * HD : (first + j + 1) * HD] for j in range(GROUP)], axis=0
    )


def forward_kernel(
    x_ref, gain_ref, wqkv_ref, wo_ref, wgu_ref, wd_ref, cos_ref, sin_ref, segc_ref, segr_ref,
    y_ref, r_ref, qkv_ref, o_ref, lse_ref,
):
    gain_a = gain_ref[0:1, :]
    gain_m = gain_ref[1:2, :]

    @pl.loop(0, BLOCKS)
    def _(index):
        rows = pl.ds(pl.multiple_of(index * BLOCK, BLOCK), BLOCK)
        x = x_ref[rows, :].astype(f32)
        normed, _ = norm(x)
        qkv = dot((normed * gain_a).astype(bf16), wqkv_ref[...])
        cosine, sine = cos_ref[rows, :], sin_ref[rows, :]
        for at in range(0, ROT, 2 * HD):
            pair = qkv[:, at : at + 2 * HD]
            turned = pair * cosine + swap_halves(pair) * sine
            if at + 2 * HD <= H * HD:
                turned = turned * score_scale
            elif at < H * HD:
                lane = lax.broadcasted_iota(jnp.int32, pair.shape, 1)
                turned = jnp.where(lane < H * HD - at, turned * score_scale, turned)
            qkv_ref[rows, at : at + 2 * HD] = turned.astype(bf16)
        qkv_ref[rows, ROT:QKV] = qkv[:, ROT:QKV].astype(bf16)

        for block in range(BLOCKS):

            @pl.when(index == block)
            def _():
                width = (block + 1) * BLOCK
                here = slice(block * BLOCK, width)
                bias = attention_bias(segc_ref[here, :], segr_ref[:, :width], block)
                for group in range(KV):
                    k_at = (H + group) * HD
                    v_at = (H + KV + group) * HD
                    queries = group_heads(qkv_ref, here, group)
                    keys = qkv_ref[0:width, k_at : k_at + HD]
                    vals = qkv_ref[0:width, v_at : v_at + HD]
                    scores = dot_cols(queries, keys).reshape(GROUP, BLOCK, width) + bias[None]
                    top = jnp.max(scores, axis=-1, keepdims=True)
                    terms = jnp.exp(scores - top)
                    total = jnp.sum(terms, axis=-1, keepdims=True)
                    mixed = dot(terms.astype(bf16).reshape(GROUP * BLOCK, width), vals)
                    mixed = mixed.reshape(GROUP, BLOCK, HD) / total
                    lse = top + jnp.log(total)
                    for j in range(GROUP):
                        head = group * GROUP + j
                        o_ref[here, head * HD : (head + 1) * HD] = mixed[j].astype(bf16)
                        lse_ref[here, head : head + 1] = lse[j]

        r = x + dot(o_ref[rows, :], wo_ref[...])
        r_ref[rows, :] = r
        normed_m, _ = norm(r)
        hidden = (normed_m * gain_m).astype(bf16)
        out = r
        for at in range(0, FF, FF_PART):
            gate = dot(hidden, wgu_ref[:, at : at + FF_PART])
            up = dot(hidden, wgu_ref[:, FF + at : FF + at + FF_PART])
            active = (gate * jax.nn.sigmoid(gate) * up).astype(bf16)
            out = out + dot(active, wd_ref[at : at + FF_PART, :])
        y_ref[rows, :] = out.astype(bf16)


def backward_kernel(
    x_ref, dy_ref, r_ref, qkv_ref, o_ref, lse_ref,
    gain_ref, wqkv_ref, wo_ref, wgu_ref, wd_ref, cos_ref, sin_ref, segc_ref, segr_ref,
    dx_ref, dgain_ref, dwqkv_ref, dwo_ref, dwgu_ref, dwd_ref,
    dqkv_acc, dob_buf, wqkv_acc, wo_acc, wgu_acc, wd_acc,
):
    gain_a = gain_ref[0:1, :]
    gain_m = gain_ref[1:2, :]
    for ref in (dgain_ref, dqkv_acc, wqkv_acc, wo_acc, wgu_acc, wd_acc):
        ref[...] = jnp.zeros(ref.shape, f32)

    @pl.loop(0, BLOCKS)
    def _(step):
        index = BLOCKS - 1 - step
        rows = pl.ds(pl.multiple_of(index * BLOCK, BLOCK), BLOCK)
        dmb = dy_ref[rows, :]
        normed_m, inverse_m = norm(r_ref[rows, :])
        hidden = (normed_m * gain_m).astype(bf16)
        dhidden = jnp.zeros((BLOCK, D), f32)
        for at in range(0, FF, FF_PART):
            cols = slice(at, at + FF_PART)
            up_cols = slice(FF + at, FF + at + FF_PART)
            gate = dot(hidden, wgu_ref[:, cols])
            up = dot(hidden, wgu_ref[:, up_cols])
            sig = jax.nn.sigmoid(gate)
            silu = gate * sig
            wd_acc[cols, :] += dot_rows((silu * up).astype(bf16), dmb)
            dactive = dot_cols(dmb, wd_ref[cols, :])
            dgate = (dactive * up * sig * (1.0 + gate * (1.0 - sig))).astype(bf16)
            dup = (dactive * silu).astype(bf16)
            wgu_acc[:, cols] += dot_rows(hidden, dgate)
            wgu_acc[:, up_cols] += dot_rows(hidden, dup)
            dhidden += dot_cols(dgate, wgu_ref[:, cols]) + dot_cols(dup, wgu_ref[:, up_cols])
        dgain_ref[1:2, :] += jnp.sum(dhidden * normed_m, axis=0, keepdims=True)
        dr = dmb.astype(f32) + norm_back(dhidden, normed_m, inverse_m, gain_m)
        drb = dr.astype(bf16)
        wo_acc[...] += dot_rows(o_ref[rows, :], drb)
        dob_buf[...] = dot_cols(drb, wo_ref[...]).astype(bf16)

        for block in range(BLOCKS):

            @pl.when(index == block)
            def _():
                width = (block + 1) * BLOCK
                here = slice(block * BLOCK, width)
                bias = attention_bias(segc_ref[here, :], segr_ref[:, :width], block)
                for group in range(KV):
                    k_at = (H + group) * HD
                    v_at = (H + KV + group) * HD
                    queries = group_heads(qkv_ref, here, group)
                    douts = group_heads(dob_buf, slice(0, BLOCK), group)
                    outs = group_heads(o_ref, here, group)
                    keys = qkv_ref[0:width, k_at : k_at + HD]
                    vals = qkv_ref[0:width, v_at : v_at + HD]
                    lse = jnp.concatenate(
                        [
                            lse_ref[here, group * GROUP + j : group * GROUP + j + 1]
                            for j in range(GROUP)
                        ],
                        axis=0,
                    ).reshape(GROUP, BLOCK, 1)
                    delta = jnp.sum(douts.astype(f32) * outs.astype(f32), axis=-1, keepdims=True)
                    scores = dot_cols(queries, keys).reshape(GROUP, BLOCK, width) + bias[None]
                    probs = jnp.exp(scores - lse).reshape(GROUP * BLOCK, width)
                    dprobs = dot_cols(douts, vals)
                    dscores = (probs * (dprobs - delta)).astype(bf16)
                    dqkv_acc[0:width, v_at : v_at + HD] += dot_rows(probs.astype(bf16), douts)
                    dqkv_acc[0:width, k_at : k_at + HD] += dot_rows(dscores, queries)
                    dq = dot(dscores, keys) * score_scale
                    for j in range(GROUP):
                        head = group * GROUP + j
                        dqkv_acc[here, head * HD : (head + 1) * HD] = dq[
                            j * BLOCK : (j + 1) * BLOCK
                        ]

        cosine, sine = cos_ref[rows, :], sin_ref[rows, :]
        parts = []
        for at in range(0, ROT, 2 * HD):
            pair = dqkv_acc[rows, at : at + 2 * HD]
            parts.append((pair * cosine - swap_halves(pair) * sine).astype(bf16))
        parts.append(dqkv_acc[rows, ROT:QKV].astype(bf16))
        dqkv = jnp.concatenate(parts, axis=1)
        normed, inverse = norm(x_ref[rows, :].astype(f32))
        wqkv_acc[...] += dot_rows((normed * gain_a).astype(bf16), dqkv)
        dhidden_a = dot_cols(dqkv, wqkv_ref[...])
        dgain_ref[0:1, :] += jnp.sum(dhidden_a * normed, axis=0, keepdims=True)
        dx_ref[rows, :] = dr + norm_back(dhidden_a, normed, inverse, gain_a)

    for out, acc in (
        (dwqkv_ref, wqkv_acc), (dwo_ref, wo_acc), (dwgu_ref, wgu_acc), (dwd_ref, wd_acc),
    ):
        out[...] = acc[...].astype(bf16)


def call(kernel, outs, scratch, flops, *operands):
    return pl.pallas_call(
        kernel,
        out_shape=[jax.ShapeDtypeStruct(shape, dtype) for shape, dtype in outs],
        in_specs=[pl.BlockSpec(memory_space=pltpu.VMEM)] * len(operands),
        out_specs=[pl.BlockSpec(memory_space=pltpu.VMEM)] * len(outs),
        scratch_shapes=[pltpu.VMEM(shape, dtype) for shape, dtype in scratch],
        compiler_params=pltpu.CompilerParams(vmem_limit_bytes=vmem_bytes),
        cost_estimate=pl.CostEstimate(
            flops=flops, bytes_accessed=20 * 2**20, transcendentals=10**7
        ),
    )(*operands)


def forward(x, weights, tables):
    return call(
        forward_kernel,
        [((LEN, D), bf16), ((LEN, D), f32), ((LEN, QKV), bf16), ((LEN, D), bf16), ((LEN, 16), f32)],
        [],
        12 * 10**9,
        x, *weights, *tables,
    )


def backward(x, dy, kept, weights, tables):
    shapes = [(D, QKV), (D, D), (D, 2 * FF), (FF, D)]
    return call(
        backward_kernel,
        [((LEN, D), f32), ((2, D), f32)] + [(shape, bf16) for shape in shapes],
        [((LEN, QKV), f32), ((BLOCK, D), bf16)] + [(shape, f32) for shape in shapes],
        40 * 10**9,
        x, dy, *kept, *weights, *tables,
    )


def swap_sections(value):
    return lax.ppermute(value, "section", [(0, 1), (1, 0)])


def gather_weight(shard, shape):
    size = shard.shape[1]
    if size % shape[1] == 0:
        part = shard.reshape(size // shape[1], shape[1])
    else:
        part = shard.reshape(size)
    own = lax.all_gather(part, "dp").reshape(shape)
    return lax.all_gather(own, "section")


def scatter_sum(grad, first_bit):
    count = lax.axis_size("dp")
    size = grad.size // count
    half = 2
    if size % grad.shape[1] == 0 and (size // grad.shape[1]) % 2 == 0:
        half = size // grad.shape[1]
    pieces = grad.reshape(count, half, size // half)
    core = lax.axis_index("section")
    low, high = pieces[:, : half // 2], pieces[:, half // 2 :]
    current = jnp.where(core == 0, low, high) + swap_sections(jnp.where(core == 0, high, low))
    bits = count.bit_length() - 1
    current = current.reshape((2,) * bits + current.shape[1:])
    place = lax.axis_index("dp")
    left = list(range(bits - 1, -1, -1))
    for turn in range(bits):
        bit = (first_bit + turn) % bits
        axis = left.index(bit)
        left.pop(axis)
        mine = (place >> bit) & 1
        kept = lax.dynamic_index_in_dim(current, mine, axis, keepdims=False)
        sent = lax.dynamic_index_in_dim(current, 1 - mine, axis, keepdims=False)
        current = kept + lax.ppermute(
            sent, "dp", [(source, source ^ (1 << bit)) for source in range(count)]
        )
    return current


def join_halves(halves):
    core = lax.axis_index("section")
    own = jnp.where(core == 0, halves[0], halves[1])
    other = swap_sections(jnp.where(core == 0, halves[1], halves[0]))
    joined = jnp.concatenate(
        [jnp.where(core == 0, own, other), jnp.where(core == 0, other, own)], axis=0
    )
    return joined.reshape(1, -1).astype(f32)


def by_section(first, second):
    core = lax.axis_index("section")
    own = jnp.where(core == 0, first, second)
    other = swap_sections(jnp.where(core == 0, second, first))
    return jnp.stack([jnp.where(core == 0, own, other), jnp.where(core == 0, other, own)])[None]


def local(ends, doc_lengths, norm_gains, w_qkv, w_out, w_gate_up, w_down):
    core = lax.axis_index("section")
    ends = ends[0]
    seqs = ends.shape[1]
    arrived = swap_sections(jnp.where(core == 0, ends[1], ends[0]))
    inputs = jnp.where(core == 0, ends[0], arrived)
    cotangents = jnp.where(core == 0, arrived, ends[1])
    lengths = lax.dynamic_index_in_dim(doc_lengths, core, 0, keepdims=False)

    gains = lax.all_gather(norm_gains, "dp", axis=1, tiled=True).reshape(2, D)
    gains = lax.all_gather(gains, "section").astype(f32)
    gathered = [
        gather_weight(w_qkv, (D, QKV)),
        gather_weight(w_out, (D, D)),
        gather_weight(w_gate_up, (D, 2 * FF)),
        gather_weight(w_down, (FF, D)),
    ]
    weights = [[gains[layer]] + [w[layer] for w in gathered] for layer in range(2)]

    tables, first_kept, second_kept, first_y, second_y = [], [], [], [], []
    for seq in range(seqs):
        segment, position = doc_layout(lengths[seq])
        tables.append((*rope_tables(position), segment[:, None], segment[None, :]))
        y0, *kept = forward(inputs[seq], weights[0], tables[seq])
        first_y.append(y0)
        first_kept.append(kept)
        y1, *kept = forward(y0, weights[1], tables[seq])
        second_y.append(y1)
        second_kept.append(kept)

    dz, dx, sums = [], [], [None, None]

    def add_up(layer, grads):
        older = sums[layer]
        sums[layer] = grads if older is None else [a + b for a, b in zip(older, grads)]

    for seq in range(seqs):
        grad, *grads = backward(
            first_y[seq], cotangents[seq], second_kept[seq], weights[1], tables[seq]
        )
        dz.append(grad)
        add_up(1, grads)
    second_halves = [scatter_sum(g, k) for k, g in enumerate(sums[1][1:])]
    for seq in range(seqs):
        grad, *grads = backward(
            inputs[seq], dz[seq].astype(bf16), first_kept[seq], weights[0], tables[seq]
        )
        dx.append(grad)
        add_up(0, grads)
    first_halves = [scatter_sum(g, k) for k, g in enumerate(sums[0][1:])]

    dgains = lax.psum(jnp.stack([sums[0][0], sums[1][0]]), ("section", "dp"))
    dgains = lax.dynamic_index_in_dim(dgains, core, 0, keepdims=False).reshape(1, -1)
    width = norm_gains.shape[1]
    dgains = lax.dynamic_slice_in_dim(dgains, lax.axis_index("dp") * width, width, 1)
    return (
        by_section(jnp.stack(first_y), jnp.stack(second_y)),
        by_section(jnp.stack(dx), jnp.stack(dz)),
        dgains,
        *[join_halves(pair) for pair in zip(first_halves, second_halves)],
    )


def solution(mesh):
    rows = P("section", None, "dp", None, None)
    shard = P("section", "dp")
    return jax.shard_map(
        local,
        mesh=mesh,
        in_specs=(rows, P(None, "dp", None)) + (shard,) * 5,
        out_specs=(rows, rows) + (shard,) * 5,
        check_vma=False,
    )
```

```python
import jax
import jax.numpy as jnp
import numpy as np
from jax import lax
from jax.experimental import pallas as pl
from jax.experimental.pallas import tpu as pltpu
from jax.sharding import PartitionSpec as P

D = 576
H = 9
KV = 3
HD = 64
FF = 1536
LEN = 1024
DOCS = 4
GROUP = H // KV
QKV = (H + 2 * KV) * HD
ROT = (H + KV) * HD
BLOCK = 256
BLOCKS = LEN // BLOCK
FF_PART = 512

norm_eps = 1e-05
rope_base = 100000.0
masked_score = -1e30
score_scale = HD ** (-0.5)
bf16 = jnp.bfloat16
f32 = jnp.float32
vmem_bytes = 60 * 2**20


def dot(left, right):
    return jnp.dot(left, right, preferred_element_type=f32)


def dot_rows(left, right):
    return lax.dot_general(left, right, (((0,), (0,)), ((), ())), preferred_element_type=f32)


def dot_cols(left, right):
    return lax.dot_general(left, right, (((1,), (1,)), ((), ())), preferred_element_type=f32)


def doc_layout(lengths):
    bounds = jnp.cumsum(lengths)
    starts = bounds - lengths
    places = jnp.arange(LEN, dtype=jnp.int32)
    segment = jnp.sum((places[:, None] >= bounds[None, :]).astype(jnp.int32), axis=1)
    onehot = (segment[:, None] == jnp.arange(DOCS, dtype=jnp.int32)[None, :]).astype(jnp.int32)
    position = places - jnp.sum(onehot * starts[None, :], axis=1)
    return (segment, position)


def rope_tables(position):
    half = HD // 2
    inverse = rope_base ** (-(jnp.arange(half, dtype=f32) * 2.0) / HD)
    angles = position.astype(f32)[:, None] * inverse
    cosine, sine = jnp.cos(angles), jnp.sin(angles)
    return (
        jnp.concatenate([cosine] * 4, axis=1),
        jnp.concatenate([-sine, sine, -sine, sine], axis=1),
    )


def norm(values):
    inverse = lax.rsqrt(jnp.mean(values * values, axis=-1, keepdims=True) + norm_eps)
    return values * inverse, inverse


def norm_back(grad, normed, inverse, gain):
    scaled = grad * gain
    return inverse * (scaled - normed * jnp.mean(scaled * normed, axis=-1, keepdims=True))


def swap_halves(pair):
    lane = lax.broadcasted_iota(jnp.int32, pair.shape, 1)
    ahead = pltpu.roll(pair, 2 * HD - HD // 2, 1)
    behind = pltpu.roll(pair, HD // 2, 1)
    return jnp.where(lane % HD < HD // 2, ahead, behind)


def attention_bias(seg_col, seg_row, block):
    width = (block + 1) * BLOCK
    rows = block * BLOCK + lax.broadcasted_iota(jnp.int32, (BLOCK, width), 0)
    cols = lax.broadcasted_iota(jnp.int32, (BLOCK, width), 1)
    allowed = (seg_col == seg_row) & (rows >= cols)
    return jnp.where(allowed, 0.0, masked_score)


def group_heads(ref, rows, group):
    first = group * GROUP
    return jnp.concatenate(
        [ref[rows, (first + j) * HD : (first + j + 1) * HD] for j in range(GROUP)], axis=0
    )


def forward_kernel(
    x_ref, gain_ref, wqkv_ref, wo_ref, wgu_ref, wd_ref, cos_ref, sin_ref, segc_ref, segr_ref,
    y_ref, r_ref, qkv_ref, o_ref, lse_ref,
):
    gain_a = gain_ref[0:1, :]
    gain_m = gain_ref[1:2, :]

    @pl.loop(0, BLOCKS)
    def _(index):
        rows = pl.ds(pl.multiple_of(index * BLOCK, BLOCK), BLOCK)
        x = x_ref[rows, :].astype(f32)
        normed, _ = norm(x)
        qkv = dot((normed * gain_a).astype(bf16), wqkv_ref[...])
        cosine, sine = cos_ref[rows, :], sin_ref[rows, :]
        for at in range(0, ROT, 2 * HD):
            pair = qkv[:, at : at + 2 * HD]
            turned = pair * cosine + swap_halves(pair) * sine
            if at + 2 * HD <= H * HD:
                turned = turned * score_scale
            elif at < H * HD:
                lane = lax.broadcasted_iota(jnp.int32, pair.shape, 1)
                turned = jnp.where(lane < H * HD - at, turned * score_scale, turned)
            qkv_ref[rows, at : at + 2 * HD] = turned.astype(bf16)
        qkv_ref[rows, ROT:QKV] = qkv[:, ROT:QKV].astype(bf16)

        for block in range(BLOCKS):

            @pl.when(index == block)
            def _():
                width = (block + 1) * BLOCK
                here = slice(block * BLOCK, width)
                bias = attention_bias(segc_ref[here, :], segr_ref[:, :width], block)
                for group in range(KV):
                    k_at = (H + group) * HD
                    v_at = (H + KV + group) * HD
                    queries = group_heads(qkv_ref, here, group)
                    keys = qkv_ref[0:width, k_at : k_at + HD]
                    vals = qkv_ref[0:width, v_at : v_at + HD]
                    scores = dot_cols(queries, keys).reshape(GROUP, BLOCK, width) + bias[None]
                    top = jnp.max(scores, axis=-1, keepdims=True)
                    terms = jnp.exp(scores - top)
                    total = jnp.sum(terms, axis=-1, keepdims=True)
                    mixed = dot(terms.astype(bf16).reshape(GROUP * BLOCK, width), vals)
                    mixed = mixed.reshape(GROUP, BLOCK, HD) / total
                    lse = top + jnp.log(total)
                    for j in range(GROUP):
                        head = group * GROUP + j
                        o_ref[here, head * HD : (head + 1) * HD] = mixed[j].astype(bf16)
                        lse_ref[here, head : head + 1] = lse[j]

        r = x + dot(o_ref[rows, :], wo_ref[...])
        r_ref[rows, :] = r
        normed_m, _ = norm(r)
        hidden = (normed_m * gain_m).astype(bf16)
        out = r
        for at in range(0, FF, FF_PART):
            gate = dot(hidden, wgu_ref[:, at : at + FF_PART])
            up = dot(hidden, wgu_ref[:, FF + at : FF + at + FF_PART])
            active = (gate * jax.nn.sigmoid(gate) * up).astype(bf16)
            out = out + dot(active, wd_ref[at : at + FF_PART, :])
        y_ref[rows, :] = out.astype(bf16)


def backward_kernel(
    x_ref, dy_ref, r_ref, qkv_ref, o_ref, lse_ref,
    gain_ref, wqkv_ref, wo_ref, wgu_ref, wd_ref, cos_ref, sin_ref, segc_ref, segr_ref,
    dx_ref, dgain_ref, dwqkv_ref, dwo_ref, dwgu_ref, dwd_ref,
    dqkv_acc, dob_buf, wqkv_acc, wo_acc, wgu_acc, wd_acc,
):
    gain_a = gain_ref[0:1, :]
    gain_m = gain_ref[1:2, :]
    for ref in (dgain_ref, dqkv_acc, wqkv_acc, wo_acc, wgu_acc, wd_acc):
        ref[...] = jnp.zeros(ref.shape, f32)

    @pl.loop(0, BLOCKS)
    def _(step):
        index = BLOCKS - 1 - step
        rows = pl.ds(pl.multiple_of(index * BLOCK, BLOCK), BLOCK)
        dmb = dy_ref[rows, :]
        normed_m, inverse_m = norm(r_ref[rows, :])
        hidden = (normed_m * gain_m).astype(bf16)
        dhidden = jnp.zeros((BLOCK, D), f32)
        for at in range(0, FF, FF_PART):
            cols = slice(at, at + FF_PART)
            up_cols = slice(FF + at, FF + at + FF_PART)
            gate = dot(hidden, wgu_ref[:, cols])
            up = dot(hidden, wgu_ref[:, up_cols])
            sig = jax.nn.sigmoid(gate)
            silu = gate * sig
            wd_acc[cols, :] += dot_rows((silu * up).astype(bf16), dmb)
            dactive = dot_cols(dmb, wd_ref[cols, :])
            dgate = (dactive * up * sig * (1.0 + gate * (1.0 - sig))).astype(bf16)
            dup = (dactive * silu).astype(bf16)
            wgu_acc[:, cols] += dot_rows(hidden, dgate)
            wgu_acc[:, up_cols] += dot_rows(hidden, dup)
            dhidden += dot_cols(dgate, wgu_ref[:, cols]) + dot_cols(dup, wgu_ref[:, up_cols])
        dgain_ref[1:2, :] += jnp.sum(dhidden * normed_m, axis=0, keepdims=True)
        dr = dmb.astype(f32) + norm_back(dhidden, normed_m, inverse_m, gain_m)
        drb = dr.astype(bf16)
        wo_acc[...] += dot_rows(o_ref[rows, :], drb)
        dob_buf[...] = dot_cols(drb, wo_ref[...]).astype(bf16)

        for block in range(BLOCKS):

            @pl.when(index == block)
            def _():
                width = (block + 1) * BLOCK
                here = slice(block * BLOCK, width)
                bias = attention_bias(segc_ref[here, :], segr_ref[:, :width], block)
                for group in range(KV):
                    k_at = (H + group) * HD
                    v_at = (H + KV + group) * HD
                    queries = group_heads(qkv_ref, here, group)
                    douts = group_heads(dob_buf, slice(0, BLOCK), group)
                    outs = group_heads(o_ref, here, group)
                    keys = qkv_ref[0:width, k_at : k_at + HD]
                    vals = qkv_ref[0:width, v_at : v_at + HD]
                    lse = jnp.concatenate(
                        [
                            lse_ref[here, group * GROUP + j : group * GROUP + j + 1]
                            for j in range(GROUP)
                        ],
                        axis=0,
                    ).reshape(GROUP, BLOCK, 1)
                    delta = jnp.sum(douts.astype(f32) * outs.astype(f32), axis=-1, keepdims=True)
                    scores = dot_cols(queries, keys).reshape(GROUP, BLOCK, width) + bias[None]
                    probs = jnp.exp(scores - lse).reshape(GROUP * BLOCK, width)
                    dprobs = dot_cols(douts, vals)
                    dscores = (probs * (dprobs - delta)).astype(bf16)
                    dqkv_acc[0:width, v_at : v_at + HD] += dot_rows(probs.astype(bf16), douts)
                    dqkv_acc[0:width, k_at : k_at + HD] += dot_rows(dscores, queries)
                    dq = dot(dscores, keys) * score_scale
                    for j in range(GROUP):
                        head = group * GROUP + j
                        dqkv_acc[here, head * HD : (head + 1) * HD] = dq[
                            j * BLOCK : (j + 1) * BLOCK
                        ]

        cosine, sine = cos_ref[rows, :], sin_ref[rows, :]
        parts = []
        for at in range(0, ROT, 2 * HD):
            pair = dqkv_acc[rows, at : at + 2 * HD]
            parts.append((pair * cosine - swap_halves(pair) * sine).astype(bf16))
        parts.append(dqkv_acc[rows, ROT:QKV].astype(bf16))
        dqkv = jnp.concatenate(parts, axis=1)
        normed, inverse = norm(x_ref[rows, :].astype(f32))
        wqkv_acc[...] += dot_rows((normed * gain_a).astype(bf16), dqkv)
        dhidden_a = dot_cols(dqkv, wqkv_ref[...])
        dgain_ref[0:1, :] += jnp.sum(dhidden_a * normed, axis=0, keepdims=True)
        dx_ref[rows, :] = dr + norm_back(dhidden_a, normed, inverse, gain_a)

    for out, acc in (
        (dwqkv_ref, wqkv_acc), (dwo_ref, wo_acc), (dwgu_ref, wgu_acc), (dwd_ref, wd_acc),
    ):
        out[...] = acc[...].astype(bf16)


def call(kernel, outs, scratch, flops, *operands):
    return pl.pallas_call(
        kernel,
        out_shape=[jax.ShapeDtypeStruct(shape, dtype) for shape, dtype in outs],
        in_specs=[pl.BlockSpec(memory_space=pltpu.VMEM)] * len(operands),
        out_specs=[pl.BlockSpec(memory_space=pltpu.VMEM)] * len(outs),
        scratch_shapes=[pltpu.VMEM(shape, dtype) for shape, dtype in scratch],
        compiler_params=pltpu.CompilerParams(vmem_limit_bytes=vmem_bytes),
        cost_estimate=pl.CostEstimate(
            flops=flops, bytes_accessed=20 * 2**20, transcendentals=10**7
        ),
    )(*operands)


def forward(x, weights, tables):
    return call(
        forward_kernel,
        [((LEN, D), bf16), ((LEN, D), f32), ((LEN, QKV), bf16), ((LEN, D), bf16), ((LEN, 16), f32)],
        [],
        12 * 10**9,
        x, *weights, *tables,
    )


def backward(x, dy, kept, weights, tables):
    shapes = [(D, QKV), (D, D), (D, 2 * FF), (FF, D)]
    return call(
        backward_kernel,
        [((LEN, D), f32), ((2, D), f32)] + [(shape, bf16) for shape in shapes],
        [((LEN, QKV), f32), ((BLOCK, D), bf16)] + [(shape, f32) for shape in shapes],
        40 * 10**9,
        x, dy, *kept, *weights, *tables,
    )


def swap_sections(value):
    return lax.ppermute(value, "section", [(0, 1), (1, 0)])


def gather_weight(shard, shape):
    size = shard.shape[1]
    if size % shape[1] == 0:
        part = shard.reshape(size // shape[1], shape[1])
    else:
        part = shard.reshape(size)
    return lax.all_gather(part, "dp").reshape(shape)


def gather_with_gains(shard, gain_shard, shape):
    size, few, width = shard.shape[1], gain_shard.shape[1], shape[1]
    rows = -(-size // width)
    part = jnp.pad(shard.reshape(size), (0, rows * width - size)).reshape(rows, width)
    gain_row = jnp.pad(gain_shard, ((0, 0), (0, width - few)))
    whole = lax.all_gather(jnp.concatenate([part, gain_row], axis=0), "dp")
    count = whole.shape[0]
    weight = whole[:, :rows]
    if size % width:
        weight = weight.reshape(count, -1)[:, :size]
    return weight.reshape(shape), whole[:, rows, :few].reshape(2, D)


def both_layers(own):
    core = lax.axis_index("section")
    other = swap_sections(own)
    return jnp.where(core == 0, own, other), jnp.where(core == 0, other, own)


def scatter_sum(grad, first_bit, gain_grad=None):
    count = lax.axis_size("dp")
    size = grad.size // count
    half = 2
    if size % grad.shape[1] == 0 and (size // grad.shape[1]) % 2 == 0:
        half = size // grad.shape[1]
    pieces = grad.reshape(count, half, size // half)
    if gain_grad is not None:
        width = size // half
        gain_rows = gain_grad.astype(bf16).reshape(count, 1, -1)
        gain_rows = jnp.pad(gain_rows, ((0, 0), (0, 0), (0, width - gain_rows.shape[2])))
        pieces = jnp.concatenate(
            [pieces[:, : half // 2], gain_rows, pieces[:, half // 2 :], gain_rows], axis=1
        )
        half = half + 2
    core = lax.axis_index("section")
    low, high = pieces[:, : half // 2], pieces[:, half // 2 :]
    current = jnp.where(core == 0, low, high) + swap_sections(jnp.where(core == 0, high, low))
    bits = count.bit_length() - 1
    current = current.reshape((2,) * bits + current.shape[1:])
    place = lax.axis_index("dp")
    left = list(range(bits - 1, -1, -1))
    for turn in range(bits):
        bit = (first_bit + turn) % bits
        axis = left.index(bit)
        left.pop(axis)
        mine = (place >> bit) & 1
        kept = lax.dynamic_index_in_dim(current, mine, axis, keepdims=False)
        sent = lax.dynamic_index_in_dim(current, 1 - mine, axis, keepdims=False)
        current = kept + lax.ppermute(
            sent, "dp", [(source, source ^ (1 << bit)) for source in range(count)]
        )
    return current


def halves_of(grads):
    gain_grad, dqkv, dout, dgate_up, ddown = grads
    return [
        scatter_sum(dqkv, 0),
        scatter_sum(dout, 1, gain_grad),
        scatter_sum(dgate_up, 2),
        scatter_sum(ddown, 3),
    ]


def join_halves(halves):
    core = lax.axis_index("section")
    own = jnp.where(core == 0, halves[0], halves[1])
    other = swap_sections(jnp.where(core == 0, halves[1], halves[0]))
    joined = jnp.concatenate(
        [jnp.where(core == 0, own, other), jnp.where(core == 0, other, own)], axis=0
    )
    return joined.astype(f32)


def by_section(first, second):
    core = lax.axis_index("section")
    own = jnp.where(core == 0, first, second)
    other = swap_sections(jnp.where(core == 0, second, first))
    return jnp.stack([jnp.where(core == 0, own, other), jnp.where(core == 0, other, own)])[None]


def local(ends, doc_lengths, norm_gains, w_qkv, w_out, w_gate_up, w_down):
    core = lax.axis_index("section")
    ends = ends[0]
    seqs = ends.shape[1]
    arrived = swap_sections(jnp.where(core == 0, ends[1], ends[0]))
    inputs = jnp.where(core == 0, ends[0], arrived)
    cotangents = jnp.where(core == 0, arrived, ends[1])
    lengths = lax.dynamic_index_in_dim(doc_lengths, core, 0, keepdims=False)

    own_out, own_gains = gather_with_gains(w_out, norm_gains, (D, D))
    own = [
        own_gains.astype(f32),
        gather_weight(w_qkv, (D, QKV)),
        own_out,
        gather_weight(w_gate_up, (D, 2 * FF)),
        gather_weight(w_down, (FF, D)),
    ]
    weights = list(zip(*[both_layers(value) for value in own]))

    tables, first_kept, second_kept, first_y, second_y = [], [], [], [], []
    for seq in range(seqs):
        segment, position = doc_layout(lengths[seq])
        tables.append((*rope_tables(position), segment[:, None], segment[None, :]))
        y0, *kept = forward(inputs[seq], weights[0], tables[seq])
        first_y.append(y0)
        first_kept.append(kept)
        y1, *kept = forward(y0, weights[1], tables[seq])
        second_y.append(y1)
        second_kept.append(kept)

    dz, dx, sums = [], [], [None, None]

    def add_up(layer, grads):
        older = sums[layer]
        sums[layer] = grads if older is None else [a + b for a, b in zip(older, grads)]

    for seq in range(seqs):
        grad, *grads = backward(
            first_y[seq], cotangents[seq], second_kept[seq], weights[1], tables[seq]
        )
        dz.append(grad)
        add_up(1, grads)
    second_halves = halves_of(sums[1])
    for seq in range(seqs):
        grad, *grads = backward(
            inputs[seq], dz[seq].astype(bf16), first_kept[seq], weights[0], tables[seq]
        )
        dx.append(grad)
        add_up(0, grads)
    first_halves = halves_of(sums[0])
    joined = [join_halves(pair) for pair in zip(first_halves, second_halves)]
    few = norm_gains.shape[1]
    half = joined[1].shape[0] // 2
    dgains = joined[1][half - 1 : half, :few]
    joined[1] = jnp.concatenate([joined[1][: half - 1], joined[1][half : 2 * half - 1]], axis=0)
    return (
        by_section(jnp.stack(first_y), jnp.stack(second_y)),
        by_section(jnp.stack(dx), jnp.stack(dz)),
        dgains,
        *[value.reshape(1, -1) for value in joined],
    )


def solution(mesh):
    rows = P("section", None, "dp", None, None)
    shard = P("section", "dp")
    return jax.shard_map(
        local,
        mesh=mesh,
        in_specs=(rows, P(None, "dp", None)) + (shard,) * 5,
        out_specs=(rows, rows) + (shard,) * 5,
        check_vma=False,
    )
```
